32 devices in a mesh: groups: 2 (over y), seq: 4 (over z), dp: 4 (over x, core).
Axes of the slice: x: 2, y: 2, z: 4, core: 2. Of those that a mesh axis runs over, the one named last changes fastest.
Arguments:
- query: bfloat16 [8, 512, 4096], P(('groups', 'dp'), 'seq'), parts along dimension 0
- key: bfloat16 [8, 512, 4096], P(('groups', 'dp'), 'seq'), parts along dimension 0
- value: bfloat16 [8, 512, 4096], P(('groups', 'dp'), 'seq'), parts along dimension 0, may hold values from -6 to 6
- grad_out: bfloat16 [8, 512, 4096], P(('groups', 'dp'), 'seq'), parts along dimension 0, may hold values from -6 to 6
- layout: int32 [32, 4, 4], replicated, may hold values from 0 to 1, as said below
- log_scale: float32 [32], replicated, may hold values from -0.3 to 0.3
Outputs:
- attended: bfloat16 [8, 512, 4096], P(('groups', 'dp'), 'seq'), parts along dimension 0
- grad_query: bfloat16 [8, 512, 4096], P(('groups', 'dp'), 'seq'), parts along dimension 0
- grad_key: bfloat16 [8, 512, 4096], P(('groups', 'dp'), 'seq'), parts along dimension 0
- grad_value: bfloat16 [8, 512, 4096], P(('groups', 'dp'), 'seq'), parts along dimension 0
- grad_log_scale: float32 [64], P('groups'), parts along dimension 0
The draws below stay inside these ranges and needn't reach their ends.
There are 2 independent parts, one for each index of `groups`. The reference program is written for one: setup_inputs(seed, part) draws one part's arguments, and reference() takes and returns one part's arrays. A program takes and returns all parts, laid end to end along the dimension named above; an argument that names none is the same for every part. Nothing has to cross between parts.
Inputs may be any that keep to these rules, and one draw needn't show every extreme that they name: layout is 0 above the block diagonal and 1 on the block diagonal and in the first block column; heads differ widely in their density of open blocks.
All inputs are finite; a program needn't handle non-finite values.
Results may differ from the reference program's by a relative error of at most 0.02.
Values may be sent and summed in bfloat16 or wider, within the bound.
A program may use at most 128 MiB of HBM per device.

```python
import math
import jax
import jax.numpy as jnp
from jax import lax

HEADS = 32
HD = 128
BLK = 128
BATCH = 4
LENGTH = 512
NBLK = 4


def shared_rows(key):
    shape = (BATCH, LENGTH, HEADS * HD)
    base = jax.random.normal(jax.random.fold_in(key, 7), shape, jnp.float32)
    return base


def draw_key(key, part):
    base = shared_rows(key)
    return base.astype(jnp.bfloat16)


def draw_query(key, part):
    key = jax.random.fold_in(key, 3)
    shape = (BATCH, LENGTH, HEADS * HD)
    return jax.random.normal(key, shape, jnp.float32).astype(jnp.bfloat16)


def draw_layout(key, part):
    key = jax.random.fold_in(key, 21)
    level = jax.random.randint(jax.random.fold_in(key, 1), (HEADS, 1, 1), 0, 7)
    picks = jax.random.randint(jax.random.fold_in(key, 2), (HEADS, NBLK, NBLK), 0, 64) < 2 ** level
    rows = jax.lax.broadcasted_iota(jnp.int32, (HEADS, NBLK, NBLK), 1)
    cols = jax.lax.broadcasted_iota(jnp.int32, (HEADS, NBLK, NBLK), 2)
    keep = (picks | (cols == rows) | (cols == 0)) & (cols <= rows)
    return keep.astype(jnp.int32)


def block_levels(key, shape, pieces, low, top_value):
    def one(dim, blocks):
        heights = jax.random.uniform(jax.random.fold_in(jax.random.fold_in(key, 6), dim), (blocks,), jnp.float32, low / len(pieces), top_value / len(pieces))
        return jnp.repeat(jnp.exp(heights), shape[dim] // blocks).reshape((-1,) + (1,) * (len(shape) - dim - 1))

    loudness = one(*pieces[0])
    for cut in pieces[1:]:
        loudness = loudness * one(*cut)
    return loudness


def bell_draw(stream_key, shape, scale, reach, cuts=(), held_as=jnp.bfloat16):
    drawn = scale * jax.random.normal(stream_key, shape, jnp.float32)
    if cuts:
        drawn = drawn * block_levels(stream_key, shape, cuts, -0.22, 0.18)
    return jnp.clip(drawn, -reach, reach).astype(held_as)


def setup_inputs(seed: int = 0, part: int = 0) -> dict:
    arg_keys = jax.random.split(jax.random.key(seed), 7)
    part_keys = jax.random.split(jax.random.fold_in(arg_keys[6], part), 7)
    query = draw_query(jax.random.fold_in(jax.random.fold_in(arg_keys[6], part), 71), part)
    key = draw_key(jax.random.fold_in(jax.random.fold_in(arg_keys[6], part), 71), part)
    value = bell_draw(part_keys[2], (BATCH, LENGTH, HEADS * HD), 1.0, 6.0, ((0, 4), (1, 4)))
    grad_out = bell_draw(part_keys[3], (BATCH, LENGTH, HEADS * HD), 1.0, 6.0, ((0, 4), (1, 4)))
    layout = draw_layout(jax.random.fold_in(arg_keys[6], 71), part)
    log_scale = jnp.clip(jax.random.uniform(arg_keys[5], (HEADS,), jnp.float32, -0.3, 0.3), -0.3, 0.3)
    return dict(query=query, key=key, value=value, grad_out=grad_out, layout=layout, log_scale=log_scale)


BIG_NEG = -1e+30

def head_pass(q, k, v, g, lay, lsc):
    length = q.shape[0]
    scale = jnp.exp(lsc) / math.sqrt(HD)
    scores = jnp.dot(q, k.T, preferred_element_type=jnp.float32) * scale
    opened = jnp.repeat(jnp.repeat(lay > 0, BLK, axis=0), BLK, axis=1)
    rows = lax.broadcasted_iota(jnp.int32, (length, length), 0)
    cols = lax.broadcasted_iota(jnp.int32, (length, length), 1)
    allowed = opened & (cols <= rows)
    masked = jnp.where(allowed, scores, BIG_NEG)
    top = lax.optimization_barrier(jnp.max(masked, axis=1))
    expo = jnp.exp(masked - top[:, None])
    total = lax.optimization_barrier(jnp.sum(expo, axis=1))
    probs = expo / total[:, None]
    probs_b = probs.astype(jnp.bfloat16)
    out = jnp.dot(probs_b, v, preferred_element_type=jnp.float32).astype(jnp.bfloat16)
    delta = lax.optimization_barrier(jnp.sum(g.astype(jnp.float32) * out.astype(jnp.float32), axis=1))
    dprobs = jnp.dot(g, v.T, preferred_element_type=jnp.float32)
    dscores = probs * (dprobs - delta[:, None])
    dls = jnp.sum(jnp.where(allowed, dscores * scores, 0.0))
    dscores_b = (dscores * scale).astype(jnp.bfloat16)
    dq = jnp.dot(dscores_b, k, preferred_element_type=jnp.float32).astype(jnp.bfloat16)
    dk = jnp.dot(dscores_b.T, q, preferred_element_type=jnp.float32).astype(jnp.bfloat16)
    dv = jnp.dot(probs_b.T, g, preferred_element_type=jnp.float32).astype(jnp.bfloat16)
    return (out, dq, dk, dv, dls)

def reference(query, key, value, grad_out, layout, log_scale):
    count = query.shape[0]
    length = query.shape[1]

    def heads_first(x):
        return x.reshape(count, length, HEADS, HD).transpose(0, 2, 1, 3).reshape(count * HEADS, length, HD)

    def tokens_first(x):
        return x.reshape(count, HEADS, length, HD).transpose(0, 2, 1, 3).reshape(count, length, HEADS * HD)
    head_ids = jnp.tile(jnp.arange(HEADS, dtype=jnp.int32), count)

    def one(item):
        q, k, v, g, h = item
        return head_pass(q, k, v, g, layout[h], log_scale[h])
    out, dq, dk, dv, dls = lax.map(one, (heads_first(query), heads_first(key), heads_first(value), heads_first(grad_out), head_ids))
    return (tokens_first(out), tokens_first(dq), tokens_first(dk), tokens_first(dv), lax.optimization_barrier(jnp.sum(dls.reshape(count, HEADS), axis=0)))
```

```python
import functools
import math

import jax
import jax.numpy as jnp
from jax import lax
from jax.experimental import pallas as pl
from jax.experimental.pallas import tpu as pltpu
from jax.sharding import PartitionSpec as P

HEADS = 32
HD = 128
BLK = 128


BIG_NEG = -1e30


def tile_scores(q_rows, k_tile, lay_sub, q_start, k_start, scale):
    rows = q_rows.shape[0]
    cols = k_tile.shape[0]
    scores = jnp.einsum("qd,kd->qk", q_rows, k_tile, preferred_element_type=jnp.float32) * scale
    opened = jnp.repeat(jnp.repeat(lay_sub > 0, BLK, axis=0), BLK, axis=1)
    pos_q = q_start + lax.broadcasted_iota(jnp.int32, (rows, cols), 0)
    pos_k = k_start + lax.broadcasted_iota(jnp.int32, (rows, cols), 1)
    allowed = opened & (pos_k <= pos_q)
    return (scores, allowed)


def layout_sub(lay, q_tile, k_tile, per_tile):
    return lax.dynamic_slice(lay, (q_tile * per_tile, k_tile * per_tile), (per_tile, per_tile))


def forward_head(q, k, v, lay, lsc, tile):
    length, width = q.shape
    steps = length // tile
    per_tile = tile // BLK
    scale = jnp.exp(lsc) / math.sqrt(HD)

    def forward_query_step(qt, carry):
        out_all, top_all, total_all = carry
        q_start = qt * tile
        q_rows = lax.dynamic_slice_in_dim(q, q_start, tile, 0)

        def stats_step(kt, state):
            sub = layout_sub(lay, qt, kt, per_tile)

            def stats_work(inner):
                top, total = inner
                k_tile = lax.dynamic_slice_in_dim(k, kt * tile, tile, 0)
                scores, allowed = tile_scores(q_rows, k_tile, sub, q_start, kt * tile, scale)
                masked = jnp.where(allowed, scores, BIG_NEG)
                newtop = jnp.maximum(top, jnp.max(masked, axis=1))
                total = total * jnp.exp(top - newtop) + jnp.sum(
                    jnp.exp(masked - newtop[:, None]), axis=1
                )
                return (newtop, total)

            return lax.cond(jnp.any(sub > 0), stats_work, lambda inner: inner, state)

        top, total = lax.fori_loop(
            0,
            qt + 1,
            stats_step,
            (jnp.full((tile,), BIG_NEG, jnp.float32), jnp.zeros((tile,), jnp.float32)),
        )

        def value_step(kt, acc):
            sub = layout_sub(lay, qt, kt, per_tile)

            def value_work(inner):
                k_tile = lax.dynamic_slice_in_dim(k, kt * tile, tile, 0)
                v_tile = lax.dynamic_slice_in_dim(v, kt * tile, tile, 0)
                scores, allowed = tile_scores(q_rows, k_tile, sub, q_start, kt * tile, scale)
                masked = jnp.where(allowed, scores, BIG_NEG)
                probs = jnp.exp(masked - top[:, None]) / total[:, None]
                return inner + jnp.dot(
                    probs.astype(jnp.bfloat16), v_tile, preferred_element_type=jnp.float32
                )

            return lax.cond(jnp.any(sub > 0), value_work, lambda inner: inner, acc)

        o_rows = lax.fori_loop(0, qt + 1, value_step, jnp.zeros((tile, width), jnp.float32)).astype(
            jnp.bfloat16
        )
        out_all = lax.dynamic_update_slice_in_dim(out_all, o_rows, q_start, 0)
        top_all = lax.dynamic_update_slice_in_dim(top_all, top, q_start, 0)
        total_all = lax.dynamic_update_slice_in_dim(total_all, total, q_start, 0)
        return (out_all, top_all, total_all)

    init = (
        jnp.zeros((length, width), jnp.bfloat16),
        jnp.zeros((length,), jnp.float32),
        jnp.zeros((length,), jnp.float32),
    )
    return lax.fori_loop(0, steps, forward_query_step, init)


def backward_head(q, k, v, g, out_all, top_all, total_all, lay, lsc, tile):
    length, width = q.shape
    steps = length // tile
    per_tile = tile // BLK
    scale = jnp.exp(lsc) / math.sqrt(HD)

    def backward_query_step(qt, carry):
        dq_all, dk_acc, dv_acc, dls = carry
        q_start = qt * tile
        q_rows = lax.dynamic_slice_in_dim(q, q_start, tile, 0)
        g_rows = lax.dynamic_slice_in_dim(g, q_start, tile, 0)
        o_rows = lax.dynamic_slice_in_dim(out_all, q_start, tile, 0)
        top = lax.dynamic_slice_in_dim(top_all, q_start, tile, 0)
        total = lax.dynamic_slice_in_dim(total_all, q_start, tile, 0)
        delta = jnp.sum(g_rows.astype(jnp.float32) * o_rows.astype(jnp.float32), axis=1)

        def key_step(kt, state):
            sub = layout_sub(lay, qt, kt, per_tile)

            def key_work(inner):
                dq_rows, dk_inner, dv_inner, dls_inner = inner
                k_start = kt * tile
                k_tile = lax.dynamic_slice_in_dim(k, k_start, tile, 0)
                v_tile = lax.dynamic_slice_in_dim(v, k_start, tile, 0)
                scores, allowed = tile_scores(q_rows, k_tile, sub, q_start, k_start, scale)
                masked = jnp.where(allowed, scores, BIG_NEG)
                probs = jnp.exp(masked - top[:, None]) / total[:, None]
                probs_b = probs.astype(jnp.bfloat16)
                dprobs = jnp.einsum("qd,kd->qk", g_rows, v_tile, preferred_element_type=jnp.float32)
                dscores = probs * (dprobs - delta[:, None])
                dls_inner = dls_inner + jnp.sum(jnp.where(allowed, dscores * scores, 0.0))
                dscores_b = (dscores * scale).astype(jnp.bfloat16)
                dq_rows = dq_rows + jnp.dot(dscores_b, k_tile, preferred_element_type=jnp.float32)
                dk_part = jnp.einsum(
                    "qk,qd->kd", dscores_b, q_rows, preferred_element_type=jnp.float32
                )
                dv_part = jnp.einsum(
                    "qk,qd->kd", probs_b, g_rows, preferred_element_type=jnp.float32
                )
                dk_inner = lax.dynamic_update_slice_in_dim(
                    dk_inner,
                    lax.dynamic_slice_in_dim(dk_inner, k_start, tile, 0) + dk_part,
                    k_start,
                    0,
                )
                dv_inner = lax.dynamic_update_slice_in_dim(
                    dv_inner,
                    lax.dynamic_slice_in_dim(dv_inner, k_start, tile, 0) + dv_part,
                    k_start,
                    0,
                )
                return (dq_rows, dk_inner, dv_inner, dls_inner)

            return lax.cond(jnp.any(sub > 0), key_work, lambda inner: inner, state)

        dq_rows, dk_acc, dv_acc, dls = lax.fori_loop(
            0, qt + 1, key_step, (jnp.zeros((tile, width), jnp.float32), dk_acc, dv_acc, dls)
        )
        dq_all = lax.dynamic_update_slice_in_dim(dq_all, dq_rows.astype(jnp.bfloat16), q_start, 0)
        return (dq_all, dk_acc, dv_acc, dls)

    init = (
        jnp.zeros((length, width), jnp.bfloat16),
        jnp.zeros((length, width), jnp.float32),
        jnp.zeros((length, width), jnp.float32),
        jnp.float32(0.0),
    )
    dq_all, dk_acc, dv_acc, dls = lax.fori_loop(0, steps, backward_query_step, init)
    return (dq_all, dk_acc.astype(jnp.bfloat16), dv_acc.astype(jnp.bfloat16), dls)


def body_by_heads(query, key, value, grad_out, layout, log_scale):
    tok_rows = query.shape[1]
    parts = lax.axis_size("seq")
    local = HEADS // parts
    first = lax.axis_index("seq") * local
    balanced = False
    head_of_slot = jnp.arange(HEADS, dtype=jnp.int32)
    my_heads = lax.dynamic_slice_in_dim(head_of_slot, first, local, 0)
    my_layout = jnp.take(layout, my_heads, axis=0)
    my_scale = jnp.take(log_scale, my_heads, axis=0)

    def by_heads(x):
        shaped = x.reshape(tok_rows, HEADS, HD)
        return shaped

    out_list, dq_list, dk_list, dv_list, dls_list = ([], [], [], [], [])
    q_heads, k_heads, v_heads, g_heads = (
        lax.all_to_all(by_heads(query), "seq", split_axis=1, concat_axis=0, tiled=True),
        lax.all_to_all(by_heads(key), "seq", split_axis=1, concat_axis=0, tiled=True),
        lax.all_to_all(by_heads(value), "seq", split_axis=1, concat_axis=0, tiled=True),
        lax.all_to_all(by_heads(grad_out), "seq", split_axis=1, concat_axis=0, tiled=True),
    )
    tile = min(512, q_heads.shape[0])
    for head in range(local):
        out_all, top_all, total_all = forward_head(
            q_heads[:, head],
            k_heads[:, head],
            v_heads[:, head],
            my_layout[head],
            my_scale[head],
            tile,
        )
        dq_all, dk_all, dv_all, dls = backward_head(
            q_heads[:, head],
            k_heads[:, head],
            v_heads[:, head],
            g_heads[:, head],
            out_all,
            top_all,
            total_all,
            my_layout[head],
            my_scale[head],
            tile,
        )
        out_list.append(out_all)
        dq_list.append(dq_all)
        dk_list.append(dk_all)
        dv_list.append(dv_all)
        dls_list.append(dls)
    stacked = (
        jnp.stack(out_list, axis=1),
        jnp.stack(dq_list, axis=1),
        jnp.stack(dk_list, axis=1),
        jnp.stack(dv_list, axis=1),
    )
    attended, grad_query, grad_key, grad_value = (
        lax.all_to_all(stacked[0], "seq", split_axis=0, concat_axis=1, tiled=True),
        lax.all_to_all(stacked[1], "seq", split_axis=0, concat_axis=1, tiled=True),
        lax.all_to_all(stacked[2], "seq", split_axis=0, concat_axis=1, tiled=True),
        lax.all_to_all(stacked[3], "seq", split_axis=0, concat_axis=1, tiled=True),
    )
    onehot = (my_heads[:, None] == jnp.arange(HEADS, dtype=jnp.int32)[None, :]).astype(jnp.float32)
    partial_grads = jnp.sum(jnp.stack(dls_list)[:, None] * onehot, axis=0)
    grad_log_scale = lax.psum(partial_grads, ("seq", "dp"))

    def flat(x):
        return x.reshape(1, tok_rows, HEADS * HD)

    return (flat(attended), flat(grad_query), flat(grad_key), flat(grad_value), grad_log_scale)


MESH = pl.DeviceIdType.MESH
GROUP = 2
LAG = 3
NT = (((1,), (1,)), ((), ()))
TN = (((0,), (0,)), ((), ()))
NN = (((1,), (0,)), ((), ()))


def mm(a, b, dims):
    return lax.dot_general(a, b, dims, preferred_element_type=jnp.float32)


def attend(q, k, v, g, mask, lsc):
    scale = jnp.exp(jnp.full((1, q.shape[0]), lsc, jnp.float32)) * (1.0 / math.sqrt(HD))
    scores = mm(k, q, NT) * scale
    masked = mask(scores)
    top = jnp.max(masked, axis=0, keepdims=True)
    expo = jnp.exp(masked - top)
    probs = expo * (1.0 / jnp.sum(expo, axis=0, keepdims=True))
    probs_b = probs.astype(jnp.bfloat16)
    out = mm(probs_b, v, TN)
    dprobs = mm(v, g, NT)
    weighed = probs * dprobs
    delta = jnp.sum(weighed, axis=0, keepdims=True)
    dscores = weighed - probs * delta
    dls = jnp.sum(dscores * scores, axis=0, keepdims=True)
    dscores_b = (dscores * scale).astype(jnp.bfloat16)
    dq = mm(dscores_b, k, TN)
    dk = mm(dscores_b, q, NN)
    dv = mm(probs_b, g, NN)
    return out, dq, dk, dv, dls


def line_kernel(
    heads, lay, lsc, q, k, v, g, o, dq, dk, dv, dls, rb, lb, rsrc, lsrc, acc, rsend, rrecv, lsend, lrecv
):
    me = lax.axis_index("seq")
    parts = 4
    right, left = lax.rem(me + 1, parts), lax.rem(me + parts - 1, parts)
    chunks = heads // GROUP
    width = GROUP * HD
    bf = jnp.bfloat16

    def cols(c):
        return pl.ds(pl.multiple_of(c * width, width), width)

    def head_cols(h):
        return pl.ds(pl.multiple_of(h * HD, HD), HD)

    def to_right(src, dst, kind, c):
        return pltpu.make_async_remote_copy(
            src_ref=src.at[:, cols(c)], dst_ref=dst.at[:, cols(c)],
            send_sem=rsend.at[kind, c], recv_sem=rrecv.at[kind, c],
            device_id={"seq": right}, device_id_type=MESH,
        )

    def to_left(src, dst, kind, c):
        return pltpu.make_async_remote_copy(
            src_ref=src.at[:, cols(c)], dst_ref=dst.at[:, cols(c)],
            send_sem=lsend.at[kind, c], recv_sem=lrecv.at[kind, c],
            device_id={"seq": left}, device_id_type=MESH,
        )

    def wait_right(kinds, c):
        for kind in range(kinds):
            to_right(rb.at[kind], rb.at[kind], kind, c).wait_recv()

    def wait_left(kinds, c):
        for kind in range(kinds):
            to_left(lb.at[kind], lb.at[kind], kind, c).wait_recv()

    def drain(rights, lefts):
        def step(c, carry):
            for kind in range(rights):
                to_right(rb.at[kind], rb.at[kind], kind, c).wait_send()
            for kind in range(lefts):
                to_left(lb.at[kind], lb.at[kind], kind, c).wait_send()
            return carry

        lax.fori_loop(0, chunks, step, 0)

    def closed(h, row, col):
        return (lay[(h * parts + row) * parts + col] - 1).astype(jnp.float32) * -BIG_NEG

    def blocks_mask(h, rows, scores):
        after = lax.broadcasted_iota(jnp.int32, (BLK, BLK), 0) > lax.broadcasted_iota(jnp.int32, (BLK, BLK), 1)
        bands = []
        for col in range(scores.shape[0] // BLK):
            line = []
            for at, row in enumerate(rows):
                block = scores[col * BLK : (col + 1) * BLK, at * BLK : (at + 1) * BLK]
                if col > row:
                    block = jnp.full((BLK, BLK), BIG_NEG, jnp.float32)
                elif col == row:
                    block = jnp.where(after, BIG_NEG, block)
                else:
                    block = block + closed(h, row, col)
                line.append(block)
            bands.append(line[0] if len(line) == 1 else jnp.concatenate(line, axis=1))
        return bands[0] if len(bands) == 1 else jnp.concatenate(bands, axis=0)

    def work(h, rows, qs, ks, vs, gs):
        def rows_of(refs):
            got = [r[:, head_cols(h)] for r in refs]
            return got[0] if len(got) == 1 else jnp.concatenate(got, axis=0)

        out = attend(
            rows_of(qs), rows_of(ks), rows_of(vs), rows_of(gs), functools.partial(blocks_mask, h, rows), lsc[h]
        )
        part = out[4][:, :HD]
        for at in range(1, len(rows)):
            part = part + out[4][:, at * HD : (at + 1) * HD]
        dls[pl.ds(h, 1), :] = part
        return out[:4]

    def block(x, at):
        return x[at * BLK : (at + 1) * BLK]

    barrier = pltpu.get_barrier_semaphore()

    @pl.when(me > 0)
    def _():
        pl.semaphore_signal(barrier, inc=1, device_id={"seq": left}, device_id_type=MESH)

    @pl.when(me < parts - 1)
    def _():
        pl.semaphore_signal(barrier, inc=1, device_id={"seq": right}, device_id_type=MESH)

    inside = (me > 0) & (me < parts - 1)

    @pl.when(inside)
    def _():
        pl.semaphore_wait(barrier, 2)

    @pl.when(jnp.logical_not(inside))
    def _():
        pl.semaphore_wait(barrier, 1)

    @pl.when(me == 0)
    def _():
        def send(c, carry):
            to_right(k, rb.at[0], 0, c).start()
            to_right(v, rb.at[1], 1, c).start()
            return carry

        lax.fori_loop(0, chunks, send, 0)

        def compute(c, carry):
            for i in range(GROUP):
                h = c * GROUP + i
                hc = head_cols(h)
                out, gq, gk, gv = work(h, (0,), (q,), (k,), (v,), (g,))
                o[:, hc] = out.astype(bf)
                dq[:, hc] = gq.astype(bf)
                acc[0, :, hc] = gk
                acc[1, :, hc] = gv
            return carry

        lax.fori_loop(0, chunks, compute, 0)

        def finish(c, carry):
            wait_left(2, c)
            cc = cols(c)
            dk[:, cc] = (acc[0, :, cc] + lb[0, :, cc].astype(jnp.float32)).astype(bf)
            dv[:, cc] = (acc[1, :, cc] + lb[1, :, cc].astype(jnp.float32)).astype(bf)
            return carry

        lax.fori_loop(0, chunks, finish, 0)
        drain(2, 0)

    @pl.when(me == 1)
    def _():
        def finish(c):
            wait_left(4, c)
            cc = cols(c)
            for kind in range(2):
                lsrc[kind, :, cc] = (acc[kind, :, cc] + lb[kind, :, cc].astype(jnp.float32)).astype(bf)
                to_left(lsrc.at[kind], lb.at[kind], kind, c).start()
            dk[:, cc] = (acc[2, :, cc] + lb[2, :, cc].astype(jnp.float32)).astype(bf)
            dv[:, cc] = (acc[3, :, cc] + lb[3, :, cc].astype(jnp.float32)).astype(bf)

        def step(c, carry):
            to_right(k, rb.at[2], 2, c).start()
            to_right(v, rb.at[3], 3, c).start()
            wait_right(2, c)
            to_right(rb.at[0], rb.at[0], 0, c).start()
            to_right(rb.at[1], rb.at[1], 1, c).start()
            for i in range(GROUP):
                h = c * GROUP + i
                hc = head_cols(h)
                out, gq, gk, gv = work(h, (1,), (q,), (rb.at[0], k), (rb.at[1], v), (g,))
                o[:, hc] = out.astype(bf)
                dq[:, hc] = gq.astype(bf)
                acc[0, :, hc] = block(gk, 0)
                acc[1, :, hc] = block(gv, 0)
                acc[2, :, hc] = block(gk, 1)
                acc[3, :, hc] = block(gv, 1)

            @pl.when(c >= LAG)
            def _():
                finish(c - LAG)

            return carry

        lax.fori_loop(0, chunks, step, 0)

        def tail(c, carry):
            finish(c)
            return carry

        lax.fori_loop(max(chunks - LAG, 0), chunks, tail, 0)
        drain(4, 2)

    @pl.when(me == 2)
    def _():
        def step(c, carry):
            wait_left(4, c)
            wait_right(4, c)
            for i in range(GROUP):
                h = c * GROUP + i
                hc = head_cols(h)
                out, gq, gk, gv = work(
                    h, (2, 3), (q, lb.at[0]), (rb.at[0], rb.at[2], k, lb.at[1]),
                    (rb.at[1], rb.at[3], v, lb.at[2]), (g, lb.at[3]),
                )
                o[:, hc] = block(out, 0).astype(bf)
                dq[:, hc] = block(gq, 0).astype(bf)
                dk[:, hc] = block(gk, 2).astype(bf)
                dv[:, hc] = block(gv, 2).astype(bf)
                rsrc[0, :, hc] = block(out, 1).astype(bf)
                rsrc[1, :, hc] = block(gq, 1).astype(bf)
                rsrc[2, :, hc] = block(gk, 3).astype(bf)
                rsrc[3, :, hc] = block(gv, 3).astype(bf)
                lsrc[0, :, hc] = block(gk, 0).astype(bf)
                lsrc[1, :, hc] = block(gv, 0).astype(bf)
                lsrc[2, :, hc] = block(gk, 1).astype(bf)
                lsrc[3, :, hc] = block(gv, 1).astype(bf)
            for kind in range(4):
                to_left(lsrc.at[kind], lb.at[kind], kind, c).start()
            for kind, dst in enumerate((o, dq, dk, dv)):
                to_right(rsrc.at[kind], dst, kind, c).start()
            return carry

        lax.fori_loop(0, chunks, step, 0)
        drain(4, 4)

    @pl.when(me == 3)
    def _():
        def send(c, carry):
            for kind, src in enumerate((q, k, v, g)):
                to_left(src, lb.at[kind], kind, c).start()
            return carry

        lax.fori_loop(0, chunks, send, 0)
        dls[...] = jnp.zeros_like(dls)

        def collect(c, carry):
            for kind, dst in enumerate((o, dq, dk, dv)):
                to_right(dst, dst, kind, c).wait_recv()
            return carry

        lax.fori_loop(0, chunks, collect, 0)
        drain(0, 4)


def body(query, key, value, grad_out, layout, log_scale):
    _, rows, features = query.shape
    heads = features // HD
    if lax.axis_size("seq") != 4 or rows != BLK or query.shape[0] != 1:
        return body_by_heads(query, key, value, grad_out, layout, log_scale)
    flat = jax.ShapeDtypeStruct((rows, features), jnp.bfloat16)
    chunks = heads // GROUP
    vmem = pl.BlockSpec(memory_space=pltpu.VMEM)
    smem = pl.BlockSpec(memory_space=pltpu.SMEM)
    landing = pltpu.VMEM((4, rows, features), jnp.bfloat16)
    sems = pltpu.SemaphoreType.DMA((4, chunks))
    out, dq, dk, dv, dls = pl.pallas_call(
        functools.partial(line_kernel, heads),
        out_shape=(flat, flat, flat, flat, jax.ShapeDtypeStruct((heads, HD), jnp.float32)),
        in_specs=[smem, smem, vmem, vmem, vmem, vmem],
        out_specs=[vmem] * 5,
        scratch_shapes=[landing] * 4
        + [pltpu.VMEM((4, rows, features), jnp.float32)]
        + [sems] * 4,
        compiler_params=pltpu.CompilerParams(
            collective_id=0, has_side_effects=True, vmem_limit_bytes=48 * 1024 * 1024
        ),
    )(
        layout.reshape(-1),
        log_scale,
        *(x.reshape(rows, features) for x in (query, key, value, grad_out)),
    )
    grad_log_scale = lax.psum(jnp.sum(dls, axis=1), ("seq", "dp"))
    return tuple(x.reshape(1, rows, features) for x in (out, dq, dk, dv)) + (grad_log_scale,)


def solution(mesh):
    return jax.shard_map(
        body,
        mesh=mesh,
        in_specs=(
            P(("groups", "dp"), "seq", None),
            P(("groups", "dp"), "seq", None),
            P(("groups", "dp"), "seq", None),
            P(("groups", "dp"), "seq", None),
            P(),
            P(),
        ),
        out_specs=(
            P(("groups", "dp"), "seq", None),
            P(("groups", "dp"), "seq", None),
            P(("groups", "dp"), "seq", None),
            P(("groups", "dp"), "seq", None),
            P("groups"),
        ),
        check_vma=False,
    )
```

```python
import functools
import math

import jax
import jax.numpy as jnp
from jax import lax
from jax.experimental import pallas as pl
from jax.experimental.pallas import tpu as pltpu
from jax.sharding import PartitionSpec as P

HEADS = 32
HD = 128
BLK = 128


BIG_NEG = -1e30


def tile_scores(q_rows, k_tile, lay_sub, q_start, k_start, scale):
    rows = q_rows.shape[0]
    cols = k_tile.shape[0]
    scores = jnp.einsum("qd,kd->qk", q_rows, k_tile, preferred_element_type=jnp.float32) * scale
    opened = jnp.repeat(jnp.repeat(lay_sub > 0, BLK, axis=0), BLK, axis=1)
    pos_q = q_start + lax.broadcasted_iota(jnp.int32, (rows, cols), 0)
    pos_k = k_start + lax.broadcasted_iota(jnp.int32, (rows, cols), 1)
    allowed = opened & (pos_k <= pos_q)
    return (scores, allowed)


def layout_sub(lay, q_tile, k_tile, per_tile):
    return lax.dynamic_slice(lay, (q_tile * per_tile, k_tile * per_tile), (per_tile, per_tile))


def forward_head(q, k, v, lay, lsc, tile):
    length, width = q.shape
    steps = length // tile
    per_tile = tile // BLK
    scale = jnp.exp(lsc) / math.sqrt(HD)

    def forward_query_step(qt, carry):
        out_all, top_all, total_all = carry
        q_start = qt * tile
        q_rows = lax.dynamic_slice_in_dim(q, q_start, tile, 0)

        def stats_step(kt, state):
            sub = layout_sub(lay, qt, kt, per_tile)

            def stats_work(inner):
                top, total = inner
                k_tile = lax.dynamic_slice_in_dim(k, kt * tile, tile, 0)
                scores, allowed = tile_scores(q_rows, k_tile, sub, q_start, kt * tile, scale)
                masked = jnp.where(allowed, scores, BIG_NEG)
                newtop = jnp.maximum(top, jnp.max(masked, axis=1))
                total = total * jnp.exp(top - newtop) + jnp.sum(
                    jnp.exp(masked - newtop[:, None]), axis=1
                )
                return (newtop, total)

            return lax.cond(jnp.any(sub > 0), stats_work, lambda inner: inner, state)

        top, total = lax.fori_loop(
            0,
            qt + 1,
            stats_step,
            (jnp.full((tile,), BIG_NEG, jnp.float32), jnp.zeros((tile,), jnp.float32)),
        )

        def value_step(kt, acc):
            sub = layout_sub(lay, qt, kt, per_tile)

            def value_work(inner):
                k_tile = lax.dynamic_slice_in_dim(k, kt * tile, tile, 0)
                v_tile = lax.dynamic_slice_in_dim(v, kt * tile, tile, 0)
                scores, allowed = tile_scores(q_rows, k_tile, sub, q_start, kt * tile, scale)
                masked = jnp.where(allowed, scores, BIG_NEG)
                probs = jnp.exp(masked - top[:, None]) / total[:, None]
                return inner + jnp.dot(
                    probs.astype(jnp.bfloat16), v_tile, preferred_element_type=jnp.float32
                )

            return lax.cond(jnp.any(sub > 0), value_work, lambda inner: inner, acc)

        o_rows = lax.fori_loop(0, qt + 1, value_step, jnp.zeros((tile, width), jnp.float32)).astype(
            jnp.bfloat16
        )
        out_all = lax.dynamic_update_slice_in_dim(out_all, o_rows, q_start, 0)
        top_all = lax.dynamic_update_slice_in_dim(top_all, top, q_start, 0)
        total_all = lax.dynamic_update_slice_in_dim(total_all, total, q_start, 0)
        return (out_all, top_all, total_all)

    init = (
        jnp.zeros((length, width), jnp.bfloat16),
        jnp.zeros((length,), jnp.float32),
        jnp.zeros((length,), jnp.float32),
    )
    return lax.fori_loop(0, steps, forward_query_step, init)


def backward_head(q, k, v, g, out_all, top_all, total_all, lay, lsc, tile):
    length, width = q.shape
    steps = length // tile
    per_tile = tile // BLK
    scale = jnp.exp(lsc) / math.sqrt(HD)

    def backward_query_step(qt, carry):
        dq_all, dk_acc, dv_acc, dls = carry
        q_start = qt * tile
        q_rows = lax.dynamic_slice_in_dim(q, q_start, tile, 0)
        g_rows = lax.dynamic_slice_in_dim(g, q_start, tile, 0)
        o_rows = lax.dynamic_slice_in_dim(out_all, q_start, tile, 0)
        top = lax.dynamic_slice_in_dim(top_all, q_start, tile, 0)
        total = lax.dynamic_slice_in_dim(total_all, q_start, tile, 0)
        delta = jnp.sum(g_rows.astype(jnp.float32) * o_rows.astype(jnp.float32), axis=1)

        def key_step(kt, state):
            sub = layout_sub(lay, qt, kt, per_tile)

            def key_work(inner):
                dq_rows, dk_inner, dv_inner, dls_inner = inner
                k_start = kt * tile
                k_tile = lax.dynamic_slice_in_dim(k, k_start, tile, 0)
                v_tile = lax.dynamic_slice_in_dim(v, k_start, tile, 0)
                scores, allowed = tile_scores(q_rows, k_tile, sub, q_start, k_start, scale)
                masked = jnp.where(allowed, scores, BIG_NEG)
                probs = jnp.exp(masked - top[:, None]) / total[:, None]
                probs_b = probs.astype(jnp.bfloat16)
                dprobs = jnp.einsum("qd,kd->qk", g_rows, v_tile, preferred_element_type=jnp.float32)
                dscores = probs * (dprobs - delta[:, None])
                dls_inner = dls_inner + jnp.sum(jnp.where(allowed, dscores * scores, 0.0))
                dscores_b = (dscores * scale).astype(jnp.bfloat16)
                dq_rows = dq_rows + jnp.dot(dscores_b, k_tile, preferred_element_type=jnp.float32)
                dk_part = jnp.einsum(
                    "qk,qd->kd", dscores_b, q_rows, preferred_element_type=jnp.float32
                )
                dv_part = jnp.einsum(
                    "qk,qd->kd", probs_b, g_rows, preferred_element_type=jnp.float32
                )
                dk_inner = lax.dynamic_update_slice_in_dim(
                    dk_inner,
                    lax.dynamic_slice_in_dim(dk_inner, k_start, tile, 0) + dk_part,
                    k_start,
                    0,
                )
                dv_inner = lax.dynamic_update_slice_in_dim(
                    dv_inner,
                    lax.dynamic_slice_in_dim(dv_inner, k_start, tile, 0) + dv_part,
                    k_start,
                    0,
                )
                return (dq_rows, dk_inner, dv_inner, dls_inner)

            return lax.cond(jnp.any(sub > 0), key_work, lambda inner: inner, state)

        dq_rows, dk_acc, dv_acc, dls = lax.fori_loop(
            0, qt + 1, key_step, (jnp.zeros((tile, width), jnp.float32), dk_acc, dv_acc, dls)
        )
        dq_all = lax.dynamic_update_slice_in_dim(dq_all, dq_rows.astype(jnp.bfloat16), q_start, 0)
        return (dq_all, dk_acc, dv_acc, dls)

    init = (
        jnp.zeros((length, width), jnp.bfloat16),
        jnp.zeros((length, width), jnp.float32),
        jnp.zeros((length, width), jnp.float32),
        jnp.float32(0.0),
    )
    dq_all, dk_acc, dv_acc, dls = lax.fori_loop(0, steps, backward_query_step, init)
    return (dq_all, dk_acc.astype(jnp.bfloat16), dv_acc.astype(jnp.bfloat16), dls)


def body_by_heads(query, key, value, grad_out, layout, log_scale):
    tok_rows = query.shape[1]
    parts = lax.axis_size("seq")
    local = HEADS // parts
    first = lax.axis_index("seq") * local
    balanced = False
    head_of_slot = jnp.arange(HEADS, dtype=jnp.int32)
    my_heads = lax.dynamic_slice_in_dim(head_of_slot, first, local, 0)
    my_layout = jnp.take(layout, my_heads, axis=0)
    my_scale = jnp.take(log_scale, my_heads, axis=0)

    def by_heads(x):
        shaped = x.reshape(tok_rows, HEADS, HD)
        return shaped

    out_list, dq_list, dk_list, dv_list, dls_list = ([], [], [], [], [])
    q_heads, k_heads, v_heads, g_heads = (
        lax.all_to_all(by_heads(query), "seq", split_axis=1, concat_axis=0, tiled=True),
        lax.all_to_all(by_heads(key), "seq", split_axis=1, concat_axis=0, tiled=True),
        lax.all_to_all(by_heads(value), "seq", split_axis=1, concat_axis=0, tiled=True),
        lax.all_to_all(by_heads(grad_out), "seq", split_axis=1, concat_axis=0, tiled=True),
    )
    tile = min(512, q_heads.shape[0])
    for head in range(local):
        out_all, top_all, total_all = forward_head(
            q_heads[:, head],
            k_heads[:, head],
            v_heads[:, head],
            my_layout[head],
            my_scale[head],
            tile,
        )
        dq_all, dk_all, dv_all, dls = backward_head(
            q_heads[:, head],
            k_heads[:, head],
            v_heads[:, head],
            g_heads[:, head],
            out_all,
            top_all,
            total_all,
            my_layout[head],
            my_scale[head],
            tile,
        )
        out_list.append(out_all)
        dq_list.append(dq_all)
        dk_list.append(dk_all)
        dv_list.append(dv_all)
        dls_list.append(dls)
    stacked = (
        jnp.stack(out_list, axis=1),
        jnp.stack(dq_list, axis=1),
        jnp.stack(dk_list, axis=1),
        jnp.stack(dv_list, axis=1),
    )
    attended, grad_query, grad_key, grad_value = (
        lax.all_to_all(stacked[0], "seq", split_axis=0, concat_axis=1, tiled=True),
        lax.all_to_all(stacked[1], "seq", split_axis=0, concat_axis=1, tiled=True),
        lax.all_to_all(stacked[2], "seq", split_axis=0, concat_axis=1, tiled=True),
        lax.all_to_all(stacked[3], "seq", split_axis=0, concat_axis=1, tiled=True),
    )
    onehot = (my_heads[:, None] == jnp.arange(HEADS, dtype=jnp.int32)[None, :]).astype(jnp.float32)
    partial_grads = jnp.sum(jnp.stack(dls_list)[:, None] * onehot, axis=0)
    grad_log_scale = lax.psum(partial_grads, ("seq", "dp"))

    def flat(x):
        return x.reshape(1, tok_rows, HEADS * HD)

    return (flat(attended), flat(grad_query), flat(grad_key), flat(grad_value), grad_log_scale)


MESH = pl.DeviceIdType.MESH
GROUP = 1
LAG = 10
AHEAD = 3
NT = (((1,), (1,)), ((), ()))
TN = (((0,), (0,)), ((), ()))
NN = (((1,), (0,)), ((), ()))


def mm(a, b, dims):
    return lax.dot_general(a, b, dims, preferred_element_type=jnp.float32)


def attend(q, k, v, g, mask, lsc):
    scale = jnp.exp(jnp.full((1, q.shape[0]), lsc, jnp.float32)) * (1.0 / math.sqrt(HD))
    scores = mm(k, q, NT) * scale
    masked = mask(scores)
    top = jnp.max(masked, axis=0, keepdims=True)
    expo = jnp.exp(masked - top)
    probs = expo * (1.0 / jnp.sum(expo, axis=0, keepdims=True))
    probs_b = probs.astype(jnp.bfloat16)
    out = mm(probs_b, v, TN)
    dprobs = mm(v, g, NT)
    weighed = probs * dprobs
    delta = jnp.sum(weighed, axis=0, keepdims=True)
    dscores = weighed - probs * delta
    dls = jnp.sum(dscores * scores, axis=0, keepdims=True)
    dscores_b = (dscores * scale).astype(jnp.bfloat16)
    dq = mm(dscores_b, k, TN)
    dk = mm(dscores_b, q, NN)
    dv = mm(probs_b, g, NN)
    return out, dq, dk, dv, dls


def line_kernel(
    heads, dps, lay, lsc, q, k, v, g, o, dq, dk, dv, dls,
    own, rb, lb, rsrc, lsrc, acc, dloc, dgot, rsend, rrecv, lsend, lrecv, dsend, drecv, isem
):
    me = lax.axis_index("seq")
    at_dp = lax.axis_index("dp")
    parts = 4
    right, left = lax.rem(me + 1, parts), lax.rem(me + parts - 1, parts)
    chunks = heads // GROUP
    width = GROUP * HD
    bf = jnp.bfloat16
    outs = (o, dq, dk, dv)
    first, second = pl.ds(0, 2), pl.ds(2, 2)

    def cols(c):
        return pl.ds(pl.multiple_of(c * width, width), width)

    def head_cols(h):
        return pl.ds(pl.multiple_of(h * HD, HD), HD)

    def to_right(src, dst, pair, c):
        return pltpu.make_async_remote_copy(
            src_ref=src, dst_ref=dst, send_sem=rsend.at[pair, c], recv_sem=rrecv.at[pair, c],
            device_id={"seq": right}, device_id_type=MESH,
        )

    def to_left(src, dst, pair, c):
        return pltpu.make_async_remote_copy(
            src_ref=src, dst_ref=dst, send_sem=lsend.at[pair, c], recv_sem=lrecv.at[pair, c],
            device_id={"seq": left}, device_id_type=MESH,
        )

    def both(buf, pair, c):
        return buf.at[second if pair else first, :, cols(c)]

    def wait_right(pairs, c):
        for pair in range(pairs):
            to_right(both(rb, pair, c), both(rb, pair, c), pair, c).wait_recv()

    def wait_left(pairs, c):
        for pair in range(pairs):
            to_left(both(lb, pair, c), both(lb, pair, c), pair, c).wait_recv()

    def drain(rights, lefts):
        def step(c, carry):
            for pair in range(rights):
                to_right(both(rb, pair, c), both(rb, pair, c), pair, c).wait_send()
            for pair in range(lefts):
                to_left(both(lb, pair, c), both(lb, pair, c), pair, c).wait_send()
            return carry

        lax.fori_loop(0, chunks, step, 0)

    def move(src, dst, send, recv, **device):
        return pltpu.make_async_remote_copy(
            src_ref=src, dst_ref=dst, send_sem=dsend.at[send], recv_sem=drecv.at[recv],
            device_id=device, device_id_type=MESH,
        )

    def total_out():
        move(dloc, dls, 0, 2, seq=2).wait_recv()

    load = [pltpu.make_async_copy(x, own.at[at], isem.at[at]) for at, x in enumerate((q, k, v, g))]
    oq, ok, ov, og = (own.at[at] for at in range(4))

    def loaded():
        for copy in load:
            copy.wait()

    def closed(h, row, col):
        return (lay[row, col, h] - 1).astype(jnp.float32) * -BIG_NEG

    def blocks_mask(h, rows, scores):
        after = lax.broadcasted_iota(jnp.int32, (BLK, BLK), 0) > lax.broadcasted_iota(jnp.int32, (BLK, BLK), 1)
        bands = []
        for col in range(scores.shape[0] // BLK):
            line = []
            for at, row in enumerate(rows):
                block = scores[col * BLK : (col + 1) * BLK, at * BLK : (at + 1) * BLK]
                if col > row:
                    block = jnp.full((BLK, BLK), BIG_NEG, jnp.float32)
                elif col == row:
                    block = jnp.where(after, BIG_NEG, block)
                else:
                    block = block + closed(h, row, col)
                line.append(block)
            bands.append(line[0] if len(line) == 1 else jnp.concatenate(line, axis=1))
        return bands[0] if len(bands) == 1 else jnp.concatenate(bands, axis=0)

    def work(h, rows, qs, ks, vs, gs):
        def rows_of(refs):
            got = [r[:, head_cols(h)] for r in refs]
            return got[0] if len(got) == 1 else jnp.concatenate(got, axis=0)

        out = attend(
            rows_of(qs), rows_of(ks), rows_of(vs), rows_of(gs), functools.partial(blocks_mask, h, rows), lsc[h]
        )
        part = out[4][:, :HD]
        for at in range(1, len(rows)):
            part = part + out[4][:, at * HD : (at + 1) * HD]
        dloc[pl.ds(h, 1), :] = part
        return out[:4]

    def block(x, at):
        return x[at * BLK : (at + 1) * BLK]

    @pl.when(me < 3)
    def _():
        for copy in load:
            copy.start()

    barrier = pltpu.get_barrier_semaphore()

    def greet(**device):
        pl.semaphore_signal(barrier, inc=1, device_id=device, device_id_type=MESH)

    @pl.when(me == 0)
    def _():
        greet(seq=1)
        greet(seq=2)
        pl.semaphore_wait(barrier, 2)

    @pl.when(me == 1)
    def _():
        greet(seq=0)
        greet(seq=2)
        pl.semaphore_wait(barrier, 2)

    @pl.when(me == 2)
    def _():
        greet(seq=0)
        greet(seq=1)
        greet(seq=3)
        for step in range(1, dps):
            greet(dp=lax.rem(at_dp + step, dps))
        pl.semaphore_wait(barrier, 3 + dps - 1)

    @pl.when(me == 3)
    def _():
        greet(seq=2)
        pl.semaphore_wait(barrier, 1)

    @pl.when(me == 0)
    def _():
        def send(c, carry):
            to_right(k.at[:, cols(c)], rb.at[0, :, cols(c)], 0, c).start()
            to_right(v.at[:, cols(c)], rb.at[1, :, cols(c)], 0, c).start()
            return carry

        lax.fori_loop(0, chunks, send, 0)
        loaded()

        def compute(c, carry):
            for i in range(GROUP):
                h = c * GROUP + i
                hc = head_cols(h)
                out, gq, gk, gv = work(h, (0,), (oq,), (ok,), (ov,), (og,))
                o[:, hc] = out.astype(bf)
                dq[:, hc] = gq.astype(bf)
                acc[0, :, hc] = gk
                acc[1, :, hc] = gv
            return carry

        lax.fori_loop(0, chunks, compute, 0)
        mine = move(dloc, dgot.at[0], 0, 0, seq=2)
        mine.start()

        def finish(c, carry):
            wait_left(1, c)
            cc = cols(c)
            dk[:, cc] = (acc[0, :, cc] + lb[0, :, cc].astype(jnp.float32)).astype(bf)
            dv[:, cc] = (acc[1, :, cc] + lb[1, :, cc].astype(jnp.float32)).astype(bf)
            return carry

        lax.fori_loop(0, chunks, finish, 0)
        drain(1, 0)
        mine.wait_send()
        total_out()

    @pl.when(me == 1)
    def _():
        def send_own(c):
            to_right(k.at[:, cols(c)], rb.at[2, :, cols(c)], 1, c).start()
            to_right(v.at[:, cols(c)], rb.at[3, :, cols(c)], 1, c).start()

        def finish(c):
            wait_left(2, c)
            cc = cols(c)
            for kind in range(2):
                lsrc[kind, :, cc] = (acc[kind, :, cc] + lb[kind, :, cc].astype(jnp.float32)).astype(bf)
            to_left(both(lsrc, 0, c), both(lb, 0, c), 0, c).start()
            dk[:, cc] = (acc[2, :, cc] + lb[2, :, cc].astype(jnp.float32)).astype(bf)
            dv[:, cc] = (acc[3, :, cc] + lb[3, :, cc].astype(jnp.float32)).astype(bf)

        ahead = min(AHEAD, chunks)
        for c in range(ahead):
            send_own(c)
        loaded()

        def step(c, carry):
            wait_right(1, c)
            to_right(both(rb, 0, c), both(rb, 0, c), 0, c).start()

            @pl.when(c + ahead < chunks)
            def _():
                send_own(c + ahead)

            for i in range(GROUP):
                h = c * GROUP + i
                hc = head_cols(h)
                out, gq, gk, gv = work(h, (1,), (oq,), (rb.at[0], ok), (rb.at[1], ov), (og,))
                o[:, hc] = out.astype(bf)
                dq[:, hc] = gq.astype(bf)
                acc[0, :, hc] = block(gk, 0)
                acc[1, :, hc] = block(gv, 0)
                acc[2, :, hc] = block(gk, 1)
                acc[3, :, hc] = block(gv, 1)

            @pl.when(c >= LAG)
            def _():
                finish(c - LAG)

            return carry

        lax.fori_loop(0, chunks, step, 0)
        mine = move(dloc, dgot.at[1], 0, 1, seq=2)
        mine.start()

        def tail(c, carry):
            finish(c)
            return carry

        lax.fori_loop(max(chunks - LAG, 0), chunks, tail, 0)
        drain(2, 1)
        mine.wait_send()
        total_out()

    @pl.when(me == 2)
    def _():
        loaded()

        def step(c, carry):
            wait_left(2, c)
            wait_right(2, c)
            for i in range(GROUP):
                h = c * GROUP + i
                hc = head_cols(h)
                out, gq, gk, gv = work(
                    h, (2, 3), (oq, lb.at[0]), (rb.at[0], rb.at[2], ok, lb.at[1]),
                    (rb.at[1], rb.at[3], ov, lb.at[2]), (og, lb.at[3]),
                )
                lsrc[0, :, hc] = block(gk, 0).astype(bf)
                lsrc[1, :, hc] = block(gv, 0).astype(bf)
                lsrc[2, :, hc] = block(gk, 1).astype(bf)
                lsrc[3, :, hc] = block(gv, 1).astype(bf)
                rsrc[0, :, hc] = block(out, 1).astype(bf)
                rsrc[1, :, hc] = block(gq, 1).astype(bf)
                rsrc[2, :, hc] = block(gk, 3).astype(bf)
                rsrc[3, :, hc] = block(gv, 3).astype(bf)
                o[:, hc] = block(out, 0).astype(bf)
                dq[:, hc] = block(gq, 0).astype(bf)
                dk[:, hc] = block(gk, 2).astype(bf)
                dv[:, hc] = block(gv, 2).astype(bf)
            for pair in range(2):
                to_left(both(lsrc, pair, c), both(lb, pair, c), pair, c).start()
            for kind, dst in enumerate(outs):
                to_right(rsrc.at[kind, :, cols(c)], dst.at[:, cols(c)], kind // 2, c).start()
            return carry

        lax.fori_loop(0, chunks, step, 0)
        for part in range(2):
            move(dloc, dgot.at[part], 0, part, seq=part).wait_recv()
        dgot[2 + at_dp] = dloc[...] + dgot[0] + dgot[1]
        crossing = [
            move(dgot.at[2 + at_dp], dgot.at[2 + at_dp], step, 2 + step, dp=lax.rem(at_dp + step, dps))
            for step in range(1, dps)
        ]
        for copy in crossing:
            copy.start()
        for copy in crossing:
            copy.wait_recv()
        total = dgot[2]
        for part in range(1, dps):
            total = total + dgot[2 + part]
        dls[...] = total
        back = [move(dls, dls, dps + at, 2, seq=part) for at, part in enumerate((0, 1, 3))]
        for copy in back:
            copy.start()
        drain(2, 2)
        for copy in crossing + back:
            copy.wait_send()

    @pl.when(me == 3)
    def _():
        def send(c, carry):
            for kind, src in enumerate((q, k, v, g)):
                to_left(src.at[:, cols(c)], lb.at[kind, :, cols(c)], kind // 2, c).start()
            return carry

        lax.fori_loop(0, chunks, send, 0)

        def collect(c, carry):
            wait_right(2, c)
            return carry

        lax.fori_loop(0, chunks, collect, 0)
        drain(0, 2)
        total_out()


def write_kernel(*refs):
    count = len(refs) // 2
    sems = refs[-1]
    copies = [pltpu.make_async_copy(refs[at], refs[count + at], sems.at[at]) for at in range(count)]
    for copy in copies:
        copy.start()
    for copy in copies:
        copy.wait()


def body(query, key, value, grad_out, layout, log_scale):
    _, rows, features = query.shape
    heads = features // HD
    if lax.axis_size("seq") != 4 or rows != BLK or query.shape[0] != 1:
        return body_by_heads(query, key, value, grad_out, layout, log_scale)
    dps = lax.axis_size("dp")
    flat = jax.ShapeDtypeStruct((rows, features), jnp.bfloat16)
    chunks = heads // GROUP
    vmem = pl.BlockSpec(memory_space=pltpu.VMEM)
    smem = pl.BlockSpec(memory_space=pltpu.SMEM)
    hbm = pl.BlockSpec(memory_space=pltpu.HBM)
    landing = pltpu.VMEM((4, rows, features), jnp.bfloat16)
    sems = pltpu.SemaphoreType.DMA((2, chunks))
    *results, dls = pl.pallas_call(
        functools.partial(line_kernel, heads, dps),
        out_shape=(flat, flat, flat, flat, jax.ShapeDtypeStruct((heads, HD), jnp.float32)),
        in_specs=[smem, smem, hbm, hbm, hbm, hbm],
        out_specs=[vmem] * 5,
        scratch_shapes=[landing] * 5
        + [
            pltpu.VMEM((4, rows, features), jnp.float32),
            pltpu.VMEM((heads, HD), jnp.float32),
            pltpu.VMEM((2 + dps, heads, HD), jnp.float32),
        ]
        + [sems] * 4
        + [
            pltpu.SemaphoreType.DMA((dps + 3,)),
            pltpu.SemaphoreType.DMA((dps + 2,)),
            pltpu.SemaphoreType.DMA((4,)),
        ],
        compiler_params=pltpu.CompilerParams(
            collective_id=0, has_side_effects=True, vmem_limit_bytes=48 * 1024 * 1024
        ),
    )(
        layout.transpose(1, 2, 0),
        log_scale,
        *(x.reshape(rows, features) for x in (query, key, value, grad_out)),
    )
    results = pl.pallas_call(
        write_kernel,
        out_shape=(flat, flat, flat, flat),
        in_specs=[vmem] * 4,
        out_specs=[hbm] * 4,
        scratch_shapes=[pltpu.SemaphoreType.DMA((4,))],
        compiler_params=pltpu.CompilerParams(vmem_limit_bytes=16 * 1024 * 1024),
    )(*results)
    return tuple(x.reshape(1, rows, features) for x in results) + (jnp.sum(dls, axis=1),)


def solution(mesh):
    return jax.shard_map(
        body,
        mesh=mesh,
        in_specs=(
            P(("groups", "dp"), "seq", None),
            P(("groups", "dp"), "seq", None),
            P(("groups", "dp"), "seq", None),
            P(("groups", "dp"), "seq", None),
            P(),
            P(),
        ),
        out_specs=(
            P(("groups", "dp"), "seq", None),
            P(("groups", "dp"), "seq", None),
            P(("groups", "dp"), "seq", None),
            P(("groups", "dp"), "seq", None),
            P("groups"),
        ),
        check_vma=False,
    )
```

```python
import functools
import math

import jax
import jax.numpy as jnp
from jax import lax
from jax.experimental import pallas as pl
from jax.experimental.pallas import tpu as pltpu
from jax.sharding import PartitionSpec as P

HEADS = 32
HD = 128
BLK = 128


BIG_NEG = -1e30


def tile_scores(q_rows, k_tile, lay_sub, q_start, k_start, scale):
    rows = q_rows.shape[0]
    cols = k_tile.shape[0]
    scores = jnp.einsum("qd,kd->qk", q_rows, k_tile, preferred_element_type=jnp.float32) * scale
    opened = jnp.repeat(jnp.repeat(lay_sub > 0, BLK, axis=0), BLK, axis=1)
    pos_q = q_start + lax.broadcasted_iota(jnp.int32, (rows, cols), 0)
    pos_k = k_start + lax.broadcasted_iota(jnp.int32, (rows, cols), 1)
    allowed = opened & (pos_k <= pos_q)
    return (scores, allowed)


def layout_sub(lay, q_tile, k_tile, per_tile):
    return lax.dynamic_slice(lay, (q_tile * per_tile, k_tile * per_tile), (per_tile, per_tile))


def forward_head(q, k, v, lay, lsc, tile):
    length, width = q.shape
    steps = length // tile
    per_tile = tile // BLK
    scale = jnp.exp(lsc) / math.sqrt(HD)

    def forward_query_step(qt, carry):
        out_all, top_all, total_all = carry
        q_start = qt * tile
        q_rows = lax.dynamic_slice_in_dim(q, q_start, tile, 0)

        def stats_step(kt, state):
            sub = layout_sub(lay, qt, kt, per_tile)

            def stats_work(inner):
                top, total = inner
                k_tile = lax.dynamic_slice_in_dim(k, kt * tile, tile, 0)
                scores, allowed = tile_scores(q_rows, k_tile, sub, q_start, kt * tile, scale)
                masked = jnp.where(allowed, scores, BIG_NEG)
                newtop = jnp.maximum(top, jnp.max(masked, axis=1))
                total = total * jnp.exp(top - newtop) + jnp.sum(
                    jnp.exp(masked - newtop[:, None]), axis=1
                )
                return (newtop, total)

            return lax.cond(jnp.any(sub > 0), stats_work, lambda inner: inner, state)

        top, total = lax.fori_loop(
            0,
            qt + 1,
            stats_step,
            (jnp.full((tile,), BIG_NEG, jnp.float32), jnp.zeros((tile,), jnp.float32)),
        )

        def value_step(kt, acc):
            sub = layout_sub(lay, qt, kt, per_tile)

            def value_work(inner):
                k_tile = lax.dynamic_slice_in_dim(k, kt * tile, tile, 0)
                v_tile = lax.dynamic_slice_in_dim(v, kt * tile, tile, 0)
                scores, allowed = tile_scores(q_rows, k_tile, sub, q_start, kt * tile, scale)
                masked = jnp.where(allowed, scores, BIG_NEG)
                probs = jnp.exp(masked - top[:, None]) / total[:, None]
                return inner + jnp.dot(
                    probs.astype(jnp.bfloat16), v_tile, preferred_element_type=jnp.float32
                )

            return lax.cond(jnp.any(sub > 0), value_work, lambda inner: inner, acc)

        o_rows = lax.fori_loop(0, qt + 1, value_step, jnp.zeros((tile, width), jnp.float32)).astype(
            jnp.bfloat16
        )
        out_all = lax.dynamic_update_slice_in_dim(out_all, o_rows, q_start, 0)
        top_all = lax.dynamic_update_slice_in_dim(top_all, top, q_start, 0)
        total_all = lax.dynamic_update_slice_in_dim(total_all, total, q_start, 0)
        return (out_all, top_all, total_all)

    init = (
        jnp.zeros((length, width), jnp.bfloat16),
        jnp.zeros((length,), jnp.float32),
        jnp.zeros((length,), jnp.float32),
    )
    return lax.fori_loop(0, steps, forward_query_step, init)


def backward_head(q, k, v, g, out_all, top_all, total_all, lay, lsc, tile):
    length, width = q.shape
    steps = length // tile
    per_tile = tile // BLK
    scale = jnp.exp(lsc) / math.sqrt(HD)

    def backward_query_step(qt, carry):
        dq_all, dk_acc, dv_acc, dls = carry
        q_start = qt * tile
        q_rows = lax.dynamic_slice_in_dim(q, q_start, tile, 0)
        g_rows = lax.dynamic_slice_in_dim(g, q_start, tile, 0)
        o_rows = lax.dynamic_slice_in_dim(out_all, q_start, tile, 0)
        top = lax.dynamic_slice_in_dim(top_all, q_start, tile, 0)
        total = lax.dynamic_slice_in_dim(total_all, q_start, tile, 0)
        delta = jnp.sum(g_rows.astype(jnp.float32) * o_rows.astype(jnp.float32), axis=1)

        def key_step(kt, state):
            sub = layout_sub(lay, qt, kt, per_tile)

            def key_work(inner):
                dq_rows, dk_inner, dv_inner, dls_inner = inner
                k_start = kt * tile
                k_tile = lax.dynamic_slice_in_dim(k, k_start, tile, 0)
                v_tile = lax.dynamic_slice_in_dim(v, k_start, tile, 0)
                scores, allowed = tile_scores(q_rows, k_tile, sub, q_start, k_start, scale)
                masked = jnp.where(allowed, scores, BIG_NEG)
                probs = jnp.exp(masked - top[:, None]) / total[:, None]
                probs_b = probs.astype(jnp.bfloat16)
                dprobs = jnp.einsum("qd,kd->qk", g_rows, v_tile, preferred_element_type=jnp.float32)
                dscores = probs * (dprobs - delta[:, None])
                dls_inner = dls_inner + jnp.sum(jnp.where(allowed, dscores * scores, 0.0))
                dscores_b = (dscores * scale).astype(jnp.bfloat16)
                dq_rows = dq_rows + jnp.dot(dscores_b, k_tile, preferred_element_type=jnp.float32)
                dk_part = jnp.einsum(
                    "qk,qd->kd", dscores_b, q_rows, preferred_element_type=jnp.float32
                )
                dv_part = jnp.einsum(
                    "qk,qd->kd", probs_b, g_rows, preferred_element_type=jnp.float32
                )
                dk_inner = lax.dynamic_update_slice_in_dim(
                    dk_inner,
                    lax.dynamic_slice_in_dim(dk_inner, k_start, tile, 0) + dk_part,
                    k_start,
                    0,
                )
                dv_inner = lax.dynamic_update_slice_in_dim(
                    dv_inner,
                    lax.dynamic_slice_in_dim(dv_inner, k_start, tile, 0) + dv_part,
                    k_start,
                    0,
                )
                return (dq_rows, dk_inner, dv_inner, dls_inner)

            return lax.cond(jnp.any(sub > 0), key_work, lambda inner: inner, state)

        dq_rows, dk_acc, dv_acc, dls = lax.fori_loop(
            0, qt + 1, key_step, (jnp.zeros((tile, width), jnp.float32), dk_acc, dv_acc, dls)
        )
        dq_all = lax.dynamic_update_slice_in_dim(dq_all, dq_rows.astype(jnp.bfloat16), q_start, 0)
        return (dq_all, dk_acc, dv_acc, dls)

    init = (
        jnp.zeros((length, width), jnp.bfloat16),
        jnp.zeros((length, width), jnp.float32),
        jnp.zeros((length, width), jnp.float32),
        jnp.float32(0.0),
    )
    dq_all, dk_acc, dv_acc, dls = lax.fori_loop(0, steps, backward_query_step, init)
    return (dq_all, dk_acc.astype(jnp.bfloat16), dv_acc.astype(jnp.bfloat16), dls)


def body_by_heads(query, key, value, grad_out, layout, log_scale):
    tok_rows = query.shape[1]
    parts = lax.axis_size("seq")
    local = HEADS // parts
    first = lax.axis_index("seq") * local
    balanced = False
    head_of_slot = jnp.arange(HEADS, dtype=jnp.int32)
    my_heads = lax.dynamic_slice_in_dim(head_of_slot, first, local, 0)
    my_layout = jnp.take(layout, my_heads, axis=0)
    my_scale = jnp.take(log_scale, my_heads, axis=0)

    def by_heads(x):
        shaped = x.reshape(tok_rows, HEADS, HD)
        return shaped

    out_list, dq_list, dk_list, dv_list, dls_list = ([], [], [], [], [])
    q_heads, k_heads, v_heads, g_heads = (
        lax.all_to_all(by_heads(query), "seq", split_axis=1, concat_axis=0, tiled=True),
        lax.all_to_all(by_heads(key), "seq", split_axis=1, concat_axis=0, tiled=True),
        lax.all_to_all(by_heads(value), "seq", split_axis=1, concat_axis=0, tiled=True),
        lax.all_to_all(by_heads(grad_out), "seq", split_axis=1, concat_axis=0, tiled=True),
    )
    tile = min(512, q_heads.shape[0])
    for head in range(local):
        out_all, top_all, total_all = forward_head(
            q_heads[:, head],
            k_heads[:, head],
            v_heads[:, head],
            my_layout[head],
            my_scale[head],
            tile,
        )
        dq_all, dk_all, dv_all, dls = backward_head(
            q_heads[:, head],
            k_heads[:, head],
            v_heads[:, head],
            g_heads[:, head],
            out_all,
            top_all,
            total_all,
            my_layout[head],
            my_scale[head],
            tile,
        )
        out_list.append(out_all)
        dq_list.append(dq_all)
        dk_list.append(dk_all)
        dv_list.append(dv_all)
        dls_list.append(dls)
    stacked = (
        jnp.stack(out_list, axis=1),
        jnp.stack(dq_list, axis=1),
        jnp.stack(dk_list, axis=1),
        jnp.stack(dv_list, axis=1),
    )
    attended, grad_query, grad_key, grad_value = (
        lax.all_to_all(stacked[0], "seq", split_axis=0, concat_axis=1, tiled=True),
        lax.all_to_all(stacked[1], "seq", split_axis=0, concat_axis=1, tiled=True),
        lax.all_to_all(stacked[2], "seq", split_axis=0, concat_axis=1, tiled=True),
        lax.all_to_all(stacked[3], "seq", split_axis=0, concat_axis=1, tiled=True),
    )
    onehot = (my_heads[:, None] == jnp.arange(HEADS, dtype=jnp.int32)[None, :]).astype(jnp.float32)
    partial_grads = jnp.sum(jnp.stack(dls_list)[:, None] * onehot, axis=0)
    grad_log_scale = lax.psum(partial_grads, ("seq", "dp"))

    def flat(x):
        return x.reshape(1, tok_rows, HEADS * HD)

    return (flat(attended), flat(grad_query), flat(grad_key), flat(grad_value), grad_log_scale)


MESH = pl.DeviceIdType.MESH
GROUP = 1
LAG = 10
AHEAD = 1
PACE = 1
NT = (((1,), (1,)), ((), ()))
TN = (((0,), (0,)), ((), ()))
NN = (((1,), (0,)), ((), ()))


def mm(a, b, dims):
    return lax.dot_general(a, b, dims, preferred_element_type=jnp.float32)


def attend(q, k, v, g, mask, lsc):
    scale = jnp.exp(jnp.full((1, q.shape[0]), lsc, jnp.float32)) * (1.0 / math.sqrt(HD))
    scores = mm(k, q, NT) * scale
    masked = mask(scores)
    top = jnp.max(masked, axis=0, keepdims=True)
    expo = jnp.exp(masked - top)
    probs = expo * (1.0 / jnp.sum(expo, axis=0, keepdims=True))
    probs_b = probs.astype(jnp.bfloat16)
    out = mm(probs_b, v, TN)
    dprobs = mm(v, g, NT)
    weighed = probs * dprobs
    delta = jnp.sum(weighed, axis=0, keepdims=True)
    dscores = weighed - probs * delta
    dls = jnp.sum(dscores * scores, axis=0, keepdims=True)
    dscores_b = (dscores * scale).astype(jnp.bfloat16)
    dq = mm(dscores_b, k, TN)
    dk = mm(dscores_b, q, NN)
    dv = mm(probs_b, g, NN)
    return out, dq, dk, dv, dls


def line_kernel(
    heads, dps, lay, lsc, q, k, v, g, o, dq, dk, dv, dls,
    own, rb, lb, rsrc, lsrc, acc, dloc, dgot, rsend, rrecv, lsend, lrecv, dsend, drecv, isem
):
    me = lax.axis_index("seq")
    at_dp = lax.axis_index("dp")
    parts = 4
    right, left = lax.rem(me + 1, parts), lax.rem(me + parts - 1, parts)
    chunks = heads // GROUP
    width = GROUP * HD
    bf = jnp.bfloat16
    outs = (o, dq, dk, dv)
    first, second = pl.ds(0, 2), pl.ds(2, 2)

    def cols(c):
        return pl.ds(pl.multiple_of(c * width, width), width)

    def head_cols(h):
        return pl.ds(pl.multiple_of(h * HD, HD), HD)

    def to_right(src, dst, pair, c):
        return pltpu.make_async_remote_copy(
            src_ref=src, dst_ref=dst, send_sem=rsend.at[pair, c], recv_sem=rrecv.at[pair, c],
            device_id={"seq": right}, device_id_type=MESH,
        )

    def to_left(src, dst, pair, c):
        return pltpu.make_async_remote_copy(
            src_ref=src, dst_ref=dst, send_sem=lsend.at[pair, c], recv_sem=lrecv.at[pair, c],
            device_id={"seq": left}, device_id_type=MESH,
        )

    def both(buf, pair, c):
        return buf.at[second if pair else first, :, cols(c)]

    def wait_right(pairs, c):
        for pair in range(pairs):
            to_right(both(rb, pair, c), both(rb, pair, c), pair, c).wait_recv()

    def wait_left(pairs, c):
        for pair in range(pairs):
            to_left(both(lb, pair, c), both(lb, pair, c), pair, c).wait_recv()

    def drain(rights, lefts):
        def step(c, carry):
            for pair in range(rights):
                to_right(both(rb, pair, c), both(rb, pair, c), pair, c).wait_send()
            for pair in range(lefts):
                to_left(both(lb, pair, c), both(lb, pair, c), pair, c).wait_send()
            return carry

        lax.fori_loop(0, chunks, step, 0)

    def move(src, dst, send, recv, **device):
        return pltpu.make_async_remote_copy(
            src_ref=src, dst_ref=dst, send_sem=dsend.at[send], recv_sem=drecv.at[recv],
            device_id=device, device_id_type=MESH,
        )

    def total_out():
        move(dloc, dls, 0, 2, seq=2).wait_recv()

    load = [pltpu.make_async_copy(x, own.at[at], isem.at[at]) for at, x in enumerate((q, k, v, g))]
    oq, ok, ov, og = (own.at[at] for at in range(4))

    def loaded():
        for copy in load:
            copy.wait()

    def closed(h, row, col):
        return (lay[row, col, h] - 1).astype(jnp.float32) * -BIG_NEG

    def blocks_mask(h, rows, scores):
        after = lax.broadcasted_iota(jnp.int32, (BLK, BLK), 0) > lax.broadcasted_iota(jnp.int32, (BLK, BLK), 1)
        bands = []
        for col in range(scores.shape[0] // BLK):
            line = []
            for at, row in enumerate(rows):
                block = scores[col * BLK : (col + 1) * BLK, at * BLK : (at + 1) * BLK]
                if col > row:
                    block = jnp.full((BLK, BLK), BIG_NEG, jnp.float32)
                elif col == row:
                    block = jnp.where(after, BIG_NEG, block)
                else:
                    block = block + closed(h, row, col)
                line.append(block)
            bands.append(line[0] if len(line) == 1 else jnp.concatenate(line, axis=1))
        return bands[0] if len(bands) == 1 else jnp.concatenate(bands, axis=0)

    def work(h, rows, qs, ks, vs, gs):
        def rows_of(refs):
            got = [r[:, head_cols(h)] for r in refs]
            return got[0] if len(got) == 1 else jnp.concatenate(got, axis=0)

        out = attend(
            rows_of(qs), rows_of(ks), rows_of(vs), rows_of(gs), functools.partial(blocks_mask, h, rows), lsc[h]
        )
        part = out[4][:, :HD]
        for at in range(1, len(rows)):
            part = part + out[4][:, at * HD : (at + 1) * HD]
        dloc[pl.ds(h, 1), :] = part
        return out[:4]

    def block(x, at):
        return x[at * BLK : (at + 1) * BLK]

    @pl.when(me < 3)
    def _():
        for copy in load:
            copy.start()

    barrier = pltpu.get_barrier_semaphore()

    def greet(**device):
        pl.semaphore_signal(barrier, inc=1, device_id=device, device_id_type=MESH)

    @pl.when(me == 0)
    def _():
        greet(seq=1)
        greet(seq=2)
        pl.semaphore_wait(barrier, 2)

    @pl.when(me == 1)
    def _():
        greet(seq=0)
        greet(seq=2)
        pl.semaphore_wait(barrier, 2)

    @pl.when(me == 2)
    def _():
        greet(seq=0)
        greet(seq=1)
        greet(seq=3)
        for step in range(1, dps):
            greet(dp=lax.rem(at_dp + step, dps))
        pl.semaphore_wait(barrier, 3 + dps - 1)

    @pl.when(me == 3)
    def _():
        greet(seq=2)
        pl.semaphore_wait(barrier, 1)

    @pl.when(me == 0)
    def _():
        def send(c, carry):
            to_right(k.at[:, cols(c)], rb.at[0, :, cols(c)], 0, c).start()
            to_right(v.at[:, cols(c)], rb.at[1, :, cols(c)], 0, c).start()
            return carry

        lax.fori_loop(0, chunks, send, 0)
        loaded()

        def compute(c, carry):
            for i in range(GROUP):
                h = c * GROUP + i
                hc = head_cols(h)
                out, gq, gk, gv = work(h, (0,), (oq,), (ok,), (ov,), (og,))
                o[:, hc] = out.astype(bf)
                dq[:, hc] = gq.astype(bf)
                acc[0, :, hc] = gk
                acc[1, :, hc] = gv
            return carry

        lax.fori_loop(0, chunks, compute, 0)
        mine = move(dloc, dgot.at[0], 0, 0, seq=2)
        mine.start()

        def finish(c, carry):
            wait_left(1, c)
            cc = cols(c)
            dk[:, cc] = (acc[0, :, cc] + lb[0, :, cc].astype(jnp.float32)).astype(bf)
            dv[:, cc] = (acc[1, :, cc] + lb[1, :, cc].astype(jnp.float32)).astype(bf)
            return carry

        drain(1, 0)
        lax.fori_loop(0, chunks, finish, 0)
        mine.wait_send()
        total_out()

    @pl.when(me == 1)
    def _():
        def send_own(c):
            to_right(k.at[:, cols(c)], rb.at[2, :, cols(c)], 1, c).start()
            to_right(v.at[:, cols(c)], rb.at[3, :, cols(c)], 1, c).start()

        def finish(c):
            wait_left(2, c)
            cc = cols(c)
            for kind in range(2):
                lsrc[kind, :, cc] = (acc[kind, :, cc] + lb[kind, :, cc].astype(jnp.float32)).astype(bf)
            to_left(both(lsrc, 0, c), both(lb, 0, c), 0, c).start()
            dk[:, cc] = (acc[2, :, cc] + lb[2, :, cc].astype(jnp.float32)).astype(bf)
            dv[:, cc] = (acc[3, :, cc] + lb[3, :, cc].astype(jnp.float32)).astype(bf)

        ahead = min(AHEAD, chunks)
        for c in range(ahead):
            send_own(c)
        loaded()

        def step(c, carry):
            wait_right(1, c)
            to_right(both(rb, 0, c), both(rb, 0, c), 0, c).start()

            @pl.when(c + ahead < chunks)
            def _():
                send_own(c + ahead)

            for i in range(GROUP):
                h = c * GROUP + i
                hc = head_cols(h)
                out, gq, gk, gv = work(h, (1,), (oq,), (rb.at[0], ok), (rb.at[1], ov), (og,))
                o[:, hc] = out.astype(bf)
                dq[:, hc] = gq.astype(bf)
                acc[0, :, hc] = block(gk, 0)
                acc[1, :, hc] = block(gv, 0)
                acc[2, :, hc] = block(gk, 1)
                acc[3, :, hc] = block(gv, 1)

            @pl.when(c >= LAG)
            def _():
                finish(c - LAG)

            return carry

        lax.fori_loop(0, chunks, step, 0)
        mine = move(dloc, dgot.at[1], 0, 1, seq=2)
        mine.start()

        def tail(c, carry):
            finish(c)
            return carry

        lax.fori_loop(max(chunks - LAG, 0), chunks, tail, 0)
        drain(2, 1)
        mine.wait_send()
        total_out()

    @pl.when(me == 2)
    def _():
        loaded()

        def step(c, carry):
            wait_left(2, c)
            wait_right(2, c)
            for i in range(GROUP):
                h = c * GROUP + i
                hc = head_cols(h)
                out, gq, gk, gv = work(
                    h, (2, 3), (oq, lb.at[0]), (rb.at[0], rb.at[2], ok, lb.at[1]),
                    (rb.at[1], rb.at[3], ov, lb.at[2]), (og, lb.at[3]),
                )
                lsrc[0, :, hc] = block(gk, 0).astype(bf)
                lsrc[1, :, hc] = block(gv, 0).astype(bf)
                lsrc[2, :, hc] = block(gk, 1).astype(bf)
                lsrc[3, :, hc] = block(gv, 1).astype(bf)
                rsrc[0, :, hc] = block(out, 1).astype(bf)
                rsrc[1, :, hc] = block(gq, 1).astype(bf)
                rsrc[2, :, hc] = block(gk, 3).astype(bf)
                rsrc[3, :, hc] = block(gv, 3).astype(bf)
                o[:, hc] = block(out, 0).astype(bf)
                dq[:, hc] = block(gq, 0).astype(bf)
                dk[:, hc] = block(gk, 2).astype(bf)
                dv[:, hc] = block(gv, 2).astype(bf)
            for pair in range(2):
                to_left(both(lsrc, pair, c), both(lb, pair, c), pair, c).start()
            for kind, dst in enumerate(outs):
                to_right(rsrc.at[kind, :, cols(c)], dst.at[:, cols(c)], kind // 2, c).start()
            return carry

        lax.fori_loop(0, chunks, step, 0)
        for part in range(2):
            move(dloc, dgot.at[part], 0, part, seq=part).wait_recv()
        dgot[2 + at_dp] = dloc[...] + dgot[0] + dgot[1]
        crossing = [
            move(dgot.at[2 + at_dp], dgot.at[2 + at_dp], step, 2 + step, dp=lax.rem(at_dp + step, dps))
            for step in range(1, dps)
        ]
        for copy in crossing:
            copy.start()
        for copy in crossing:
            copy.wait_recv()
        total = dgot[2]
        for part in range(1, dps):
            total = total + dgot[2 + part]
        dls[...] = total
        back = [move(dls, dls, dps + at, 2, seq=part) for at, part in enumerate((0, 1, 3))]
        for copy in back:
            copy.start()
        drain(2, 2)
        for copy in crossing + back:
            copy.wait_send()

    @pl.when(me == 3)
    def _():
        def send(c, carry):
            for kind, src in enumerate((q, k, v, g)):
                to_left(src.at[:, cols(c)], lb.at[kind, :, cols(c)], kind // 2, c).start()

            @pl.when(c >= PACE)
            def _():
                sent(c - PACE)

            return carry

        def sent(c):
            for pair in range(2):
                to_left(both(lb, pair, c), both(lb, pair, c), pair, c).wait_send()

        lax.fori_loop(0, chunks, send, 0)
        for c in range(max(chunks - PACE, 0), chunks):
            sent(c)

        def collect(c, carry):
            wait_right(2, c)
            return carry

        lax.fori_loop(0, chunks, collect, 0)
        total_out()


def write_kernel(*refs):
    count = len(refs) // 2
    sems = refs[-1]
    copies = [pltpu.make_async_copy(refs[at], refs[count + at], sems.at[at]) for at in range(count)]
    for copy in copies:
        copy.start()
    for copy in copies:
        copy.wait()


def body(query, key, value, grad_out, layout, log_scale):
    _, rows, features = query.shape
    heads = features // HD
    if lax.axis_size("seq") != 4 or rows != BLK or query.shape[0] != 1:
        return body_by_heads(query, key, value, grad_out, layout, log_scale)
    dps = lax.axis_size("dp")
    flat = jax.ShapeDtypeStruct((rows, features), jnp.bfloat16)
    chunks = heads // GROUP
    vmem = pl.BlockSpec(memory_space=pltpu.VMEM)
    smem = pl.BlockSpec(memory_space=pltpu.SMEM)
    hbm = pl.BlockSpec(memory_space=pltpu.HBM)
    landing = pltpu.VMEM((4, rows, features), jnp.bfloat16)
    sems = pltpu.SemaphoreType.DMA((2, chunks))
    *results, dls = pl.pallas_call(
        functools.partial(line_kernel, heads, dps),
        out_shape=(flat, flat, flat, flat, jax.ShapeDtypeStruct((heads, HD), jnp.float32)),
        in_specs=[smem, smem, hbm, hbm, hbm, hbm],
        out_specs=[vmem] * 5,
        scratch_shapes=[landing] * 5
        + [
            pltpu.VMEM((4, rows, features), jnp.float32),
            pltpu.VMEM((heads, HD), jnp.float32),
            pltpu.VMEM((2 + dps, heads, HD), jnp.float32),
        ]
        + [sems] * 4
        + [
            pltpu.SemaphoreType.DMA((dps + 3,)),
            pltpu.SemaphoreType.DMA((dps + 2,)),
            pltpu.SemaphoreType.DMA((4,)),
        ],
        compiler_params=pltpu.CompilerParams(
            collective_id=0, has_side_effects=True, vmem_limit_bytes=96 * 512 * 1024
        ),
    )(
        layout.transpose(1, 2, 0),
        log_scale,
        *(x.reshape(rows, features) for x in (query, key, value, grad_out)),
    )
    results = pl.pallas_call(
        write_kernel,
        out_shape=(flat, flat, flat, flat),
        in_specs=[vmem] * 4,
        out_specs=[hbm] * 4,
        scratch_shapes=[pltpu.SemaphoreType.DMA((4,))],
        compiler_params=pltpu.CompilerParams(vmem_limit_bytes=16 * 1024 * 1024),
    )(*results)
    return tuple(x.reshape(1, rows, features) for x in results) + (jnp.sum(dls, axis=1),)


def solution(mesh):
    return jax.shard_map(
        body,
        mesh=mesh,
        in_specs=(
            P(("groups", "dp"), "seq", None),
            P(("groups", "dp"), "seq", None),
            P(("groups", "dp"), "seq", None),
            P(("groups", "dp"), "seq", None),
            P(),
            P(),
        ),
        out_specs=(
            P(("groups", "dp"), "seq", None),
            P(("groups", "dp"), "seq", None),
            P(("groups", "dp"), "seq", None),
            P(("groups", "dp"), "seq", None),
            P("groups"),
        ),
        check_vma=False,
    )
```
